256 devices in a mesh: dp: 2 (over y_lo), expert: 8 (over x, y_hi), etp: 16 (over z, core).
Axes of the slice: x: 4, y: 4 (y_hi: 2, y_lo: 2; y = y_hi * 2 + y_lo), z: 8, core: 2. Of those that a mesh axis runs over, the one named last changes fastest.
Arguments:
- tokens: bfloat16 [2048, 6144], P(('dp', 'expert'), 'etp'), may hold values from -6 to 6
- routes: int32 [2048, 2], P(('dp', 'expert')), may hold values from 0 to 7, all different within a row; in each aligned block of 128 rows (0 to 127, 128 to 255, ...) at most 48 rows name the same one
- w_gate: bfloat16 [8, 6144, 8192], P('expert', 'dp', 'etp'), may hold values from -0.078125 to 0.078125
- w_up: bfloat16 [8, 6144, 8192], P('expert', 'dp', 'etp'), may hold values from -0.078125 to 0.078125
- slot_grad: bfloat16 [2, 8, 8, 48, 8192], P('dp', 'expert', None, None, 'etp'), may hold values from -1.5 to 1.5
Outputs:
- token_grad: bfloat16 [2048, 6144], P(('dp', 'expert'), 'etp')
- gate_grad: bfloat16 [8, 6144, 8192], P('expert', 'dp', 'etp')
- up_grad: bfloat16 [8, 6144, 8192], P('expert', 'dp', 'etp')
The draws below stay inside these ranges and needn't reach their ends.
Inputs may be any that keep to these rules, and one draw needn't show every extreme that they name: `routes`: each token names 2 different experts. Among the tokens of one source no expert is named more than 48 times, and in every draw the tokens of some source name some expert exactly 48 times.
All inputs are finite; a program needn't handle non-finite values.
Results may differ from the reference program's by a relative error of at most 0.025.
Values may be sent and summed in bfloat16 or wider, within the bound.
A program may use at most 128 MiB of HBM per device.

```python
import math
import jax
import jax.numpy as jnp
import numpy as np
from jax import lax

D = 6144
FF = 8192
TOP = 2
TOK_DEV = 128
EXPERTS = 8
CAP = 48
TOKENS = 2048
N_DP = 2
N_EXPERT = 8


def block_scale(key, shape, pieces, low, top_value):
    gain = 1.0
    for position, parts in pieces:
        heights = jax.random.uniform(jax.random.fold_in(jax.random.fold_in(key, 6), position), (parts,), jnp.float32, low / len(pieces), top_value / len(pieces))
        gain = gain * jnp.repeat(jnp.exp(heights), shape[position] // parts).reshape((-1,) + (1,) * (len(shape) - 1 - position))
    return gain


def deal_out(own_key, own, number, rows, count, top, reach, slope):
    ranking = jax.random.permutation(own_key, count)
    packed, ordinary = shares(count, rows * top, reach, slope, True), shares(count, rows * top, reach, slope, False)
    places = jnp.arange(count)

    def named(sizes, offset_by):
        used = int((sizes > 0).sum())
        fixed = max(1, used // 4)
        moved = fixed + (places - fixed + offset_by * (used - fixed)) % max(1, count - fixed)
        return jnp.zeros((count,), jnp.int32).at[ranking[jnp.where(places < fixed, places, moved)]].set(jnp.asarray(sizes, jnp.int32))

    sizes = jnp.where(number % 4 == 0, named(packed, number // 4), named(ordinary, number - number // 4 - 1))
    mixed = jax.random.permutation(jax.random.fold_in(own, 3), count)
    source_of, receiver = mixed[0:count // 2 * 2:2], mixed[1:count // 2 * 2:2]
    slack = jnp.minimum(sizes[source_of] - 1, reach - sizes[receiver]) // 2
    slack = jnp.where((source_of == ranking[0]) | (receiver == ranking[0]) | (sizes[receiver] == 0), 0, jnp.maximum(slack, 0))
    moved = jax.random.randint(jax.random.fold_in(own, 4), (count // 2,), 0, 1 << 20) % (slack + 1)
    sizes = sizes.at[source_of].add(-moved).at[receiver].add(moved)
    members = jnp.searchsorted(jnp.cumsum(sizes), jnp.arange(rows * top), side="right").astype(jnp.int32)
    table = members.reshape(top, rows).T
    table = table[jax.random.permutation(jax.random.fold_in(own, 1), rows)]
    offset_by = jax.random.randint(jax.random.fold_in(own, 2), (rows, 1), 0, top)
    return jnp.take_along_axis(table, (jnp.arange(top)[None, :] + offset_by) % top, axis=1)


def shares(count, total, most, lean, full):
    portions = [(1 << 20) // math.isqrt(grade ** lean) + 1 for grade in range(1, count + 1)]
    largest = most if full else min(most, max(-(-total // count), total * portions[0] // sum(portions)))
    least = 1 if total - largest >= count - 1 else 0
    given, spare = [largest] + [least] * (count - 1), total - largest - least * (count - 1)
    while spare > 0:
        free = [i for i in range(1, count) if given[i] < largest] or [i for i in range(1, count) if given[i] < most]
        pool, budget = sum([portions[i] for i in free]), spare
        for i in free:
            addition = min(most - given[i], max(1, budget * portions[i] // pool), spare)
            given[i] = given[i] + addition
            spare = spare - addition
    return np.array(given)


def gaussian(stream_key, shape, deviation, bound, split=(), kind=jnp.bfloat16):
    values = deviation * jax.random.normal(stream_key, shape, jnp.float32)
    if split:
        values = values * block_scale(stream_key, shape, split, -0.22, 0.18)
    return jnp.clip(values, -bound, bound).astype(kind)


def setup_inputs(seed: int = 0) -> dict:
    key_list = jax.random.split(jax.random.key(seed), 6)
    tokens = gaussian(key_list[0], (TOKENS, D), 1.0, 6.0, ((0, 16), (1, 16)))
    routes_keys = jax.random.split(jax.random.fold_in(key_list[1], 1), TOKENS // TOK_DEV)
    routes_turns = jax.random.permutation(jax.random.fold_in(key_list[1], 3), TOKENS // TOK_DEV)
    routes = jax.vmap(lambda own, number: deal_out(jax.random.fold_in(key_list[1], 2), own, number, TOK_DEV, EXPERTS, TOP, CAP, 2))(routes_keys, routes_turns).reshape((TOKENS, TOP))
    w_gate = gaussian(key_list[2], (EXPERTS, D, FF), D ** -0.5, 0.078125, ((0, 8), (1, 2), (2, 16)))
    w_up = gaussian(key_list[3], (EXPERTS, D, FF), D ** -0.5, 0.078125, ((0, 8), (1, 2), (2, 16)))
    slot_grad = gaussian(key_list[4], (N_DP, EXPERTS, N_EXPERT, CAP, FF), 0.25, 1.5, ((0, 2), (1, 8), (4, 16)))
    return dict(tokens=tokens, routes=routes, w_gate=w_gate, w_up=w_up, slot_grad=slot_grad)


def slot_table(routes):
    pairs = routes.reshape(N_DP, N_EXPERT, TOK_DEV * TOP)
    onehot = (pairs[..., None] == jnp.arange(EXPERTS, dtype=jnp.int32)).astype(jnp.int32)
    before = jnp.cumsum(onehot, axis=-2) - onehot
    slot = jnp.sum(before * onehot, axis=-1)
    target = pairs * CAP + slot
    place = (target[..., None] == jnp.arange(EXPERTS * CAP, dtype=jnp.int32)).astype(jnp.float32)
    return place.reshape(N_DP, N_EXPERT, TOK_DEV, TOP, EXPERTS * CAP).sum(axis=3)


def reference(tokens, routes, w_gate, w_up, slot_grad):
    token_of = slot_table(routes)
    blocks = tokens.astype(jnp.float32).reshape(N_DP, N_EXPERT, TOK_DEV, D)
    spread = jnp.einsum('abks,abkd->absd', token_of, blocks, precision=lax.Precision.HIGHEST)
    spread = spread.reshape(N_DP, N_EXPERT, EXPERTS, CAP, D).transpose(0, 2, 1, 3, 4)
    rows = spread.reshape(N_DP, EXPERTS, N_EXPERT * CAP, D).astype(jnp.bfloat16)
    grads = slot_grad.reshape(N_DP, EXPERTS, N_EXPERT * CAP, FF)

    def expert_pass(index):
        wg = lax.dynamic_index_in_dim(w_gate, index, 0, keepdims=False)
        wu = lax.dynamic_index_in_dim(w_up, index, 0, keepdims=False)
        x_all = lax.dynamic_index_in_dim(rows, index, 1, keepdims=False)
        g_all = lax.dynamic_index_in_dim(grads, index, 1, keepdims=False)
        gate_sum = jnp.zeros((D, FF), jnp.float32)
        up_sum = jnp.zeros((D, FF), jnp.float32)
        inputs = []
        for replica in range(N_DP):
            x_rows = x_all[replica]
            grad_rows = g_all[replica].astype(jnp.float32)
            gate = jnp.dot(x_rows, wg, preferred_element_type=jnp.float32)
            up = jnp.dot(x_rows, wu, preferred_element_type=jnp.float32)
            sig = jax.nn.sigmoid(gate)
            d_gate = (grad_rows * up * sig * (1.0 + gate * (1.0 - sig))).astype(jnp.bfloat16)
            d_up = (grad_rows * gate * sig).astype(jnp.bfloat16)
            slot_input = jnp.dot(d_gate, wg.T, preferred_element_type=jnp.float32) + jnp.dot(d_up, wu.T, preferred_element_type=jnp.float32)
            inputs.append(slot_input.astype(jnp.bfloat16))
            part_gate = jnp.dot(x_rows.T, d_gate, preferred_element_type=jnp.float32).astype(jnp.bfloat16)
            part_up = jnp.dot(x_rows.T, d_up, preferred_element_type=jnp.float32).astype(jnp.bfloat16)
            gate_sum = gate_sum + lax.optimization_barrier(part_gate).astype(jnp.float32)
            up_sum = up_sum + lax.optimization_barrier(part_up).astype(jnp.float32)
        return jnp.stack(inputs), gate_sum.astype(jnp.bfloat16), up_sum.astype(jnp.bfloat16)

    slot_input, gate_grad, up_grad = lax.map(expert_pass, jnp.arange(EXPERTS, dtype=jnp.int32))
    back = slot_input.reshape(EXPERTS, N_DP, N_EXPERT, CAP, D).transpose(1, 2, 0, 3, 4)
    back = back.reshape(N_DP, N_EXPERT, EXPERTS * CAP, D).astype(jnp.float32)
    token_grad = jnp.einsum('abks,absd->abkd', token_of, back, precision=lax.Precision.HIGHEST)
    token_grad = token_grad.reshape(TOKENS, D).astype(jnp.bfloat16)
    return token_grad, gate_grad, up_grad
```

```python
import functools

import jax
import jax.numpy as jnp
from jax import lax
from jax.experimental import pallas as pl
from jax.experimental.pallas import tpu as pltpu
from jax.sharding import PartitionSpec as P

MESH = pl.DeviceIdType.MESH
F32 = jnp.float32
BF16 = jnp.bfloat16

TAU = 2
LAG_Y1 = 2
LAG_Y2 = 2
LAG_RS = 1


def tile_of(size, most):
    return most if size % most == 0 else size


def kernel(
    outgoing, w_gate, w_up, slot_grad, token_of,
    token_grad, gate_grad, up_grad,
    w_v, rows, part, y_out, y_in, d_v, g_v, g_in, rs_out, rs_in, fin, ret, dw_v,
    w_sem, dw_sem, disp_send, disp_recv, ag_send, ag_recv, sib_send, sib_recv,
    y1_send, y1_recv, y2_send, y2_recv, g_send, g_recv, rs_send, rs_recv, ret_send, ret_recv,
):
    experts, cap, feat = outgoing.shape
    depth, hidden = w_gate.shape
    chips = depth // feat
    half = chips // 2
    r = lax.axis_index("dp")
    x = lax.axis_index("expert")
    m = lax.axis_index("etp")
    z = m // 2
    c = m % 2
    base = r * half
    home = z // half
    own = home == r
    zi = z - base
    sibling = (r, x, z * 2 + 1 - c)
    partner = (1 - r, x, m)
    ring = (
        (r, x, ((z + 1) % chips) * 2 + c),
        (r, x, ((z + chips - 1) % chips) * 2 + c),
    )

    def local_wait(ref, sem):
        pltpu.make_async_copy(ref, ref, sem).wait()

    def send(src, dst, send_sem, recv_sem, device):
        pltpu.make_async_remote_copy(
            src_ref=src, dst_ref=dst, send_sem=send_sem, recv_sem=recv_sem,
            device_id=device, device_id_type=MESH,
        ).start()

    load_gate = pltpu.make_async_copy(w_gate, w_v.at[:, pl.ds(0, hidden)], w_sem.at[0])
    load_up = pltpu.make_async_copy(w_up, w_v.at[:, pl.ds(hidden, hidden)], w_sem.at[1])
    load_gate.start()
    load_up.start()

    barrier = pltpu.get_barrier_semaphore()
    for device in ring + (sibling, partner):
        pl.semaphore_signal(barrier, inc=1, device_id=device, device_id_type=MESH)

    def greet(step, carry):
        there = (x + step) % experts
        for rr in range(2):
            pl.semaphore_signal(barrier, inc=1, device_id=(rr, there, m), device_id_type=MESH)
        return carry

    lax.fori_loop(1, experts, greet, 0)
    pl.semaphore_wait(barrier, 2 * (experts - 1) + 4)

    home_block = pl.ds(pl.multiple_of((m - home * chips) * feat, 128), feat)

    def dispatch(k, carry):
        there = (x + experts - k) % experts
        dst = rows.at[k, pl.ds(pl.multiple_of(r * cap, 16), cap), home_block]
        to_self = jnp.logical_and(own, k == 0)

        @pl.when(to_self)
        def _():
            pltpu.make_async_copy(outgoing.at[there], dst, disp_recv.at[k, r]).start()

        @pl.when(jnp.logical_not(to_self))
        def _():
            send(outgoing.at[there], dst, disp_send, disp_recv.at[k, r], (home, there, m))

        return carry

    lax.fori_loop(0, experts, dispatch, 0)

    def gather_hop(k, d, sub):
        source = (z + chips - d) % chips if sub == 0 else (z + d) % chips
        i = source - base

        @pl.when(jnp.logical_and(i >= 0, i < half))
        def _():
            block = rows.at[
                k, pl.ds(sub * cap, cap), pl.ds(pl.multiple_of((2 * i + c) * feat, 128), feat)
            ]

            @pl.when(d == 0)
            def _():
                local_wait(block, disp_recv.at[k, sub])

            @pl.when(d > 0)
            def _():
                local_wait(block, ag_recv.at[k, sub, i])

            @pl.when(d < chips - 1)
            def _():
                send(block, block, ag_send.at[sub], ag_recv.at[k, sub, i], ring[sub])

            send(block, block, sib_send, sib_recv.at[k], sibling)

    def reduce_hop(k, d, sub):
        target = (z + 2 * chips - 1 - d) % chips if sub == 0 else (z + 1 + d) % chips
        i = target - base

        @pl.when(jnp.logical_and(i >= 0, i < half))
        def _():
            here = pl.ds(sub * cap, cap)
            column = pl.ds(pl.multiple_of((2 * i + c) * feat, 128), feat)
            packed = pl.ds(pl.multiple_of(i * feat, 128), feat)
            total = g_v[k, here, column].astype(F32) + g_in[k, here, packed].astype(F32)

            @pl.when(d == 0)
            def _():
                rs_out[k, sub, i] = total.astype(BF16)

            @pl.when(d > 0)
            def _():
                local_wait(rs_in.at[k, sub, i], rs_recv.at[k, sub, i])
                rs_out[k, sub, i] = (total + rs_in[k, sub, i].astype(F32)).astype(BF16)

            @pl.when(d < chips - 1)
            def _():
                send(
                    rs_out.at[k, sub, i], rs_in.at[k, sub, i],
                    rs_send, rs_recv.at[k, sub, i], ring[sub],
                )

            @pl.when(d == chips - 1)
            def _():
                there = (x + k) % experts
                to_self = jnp.logical_and(r == sub, k == 0)

                @pl.when(to_self)
                def _():
                    pltpu.make_async_copy(rs_out.at[k, sub, i], ret.at[x], ret_recv.at[x]).start()

                @pl.when(jnp.logical_not(to_self))
                def _():
                    send(rs_out.at[k, sub, i], ret.at[x], ret_send, ret_recv.at[x], (sub, there, m))

    mine = pl.ds(pl.multiple_of(r * cap, 16), cap)
    other = pl.ds(pl.multiple_of((1 - r) * cap, 16), cap)
    wide = 2 * hidden
    fwd_tile = tile_of(wide, 256)
    dx_tile = tile_of(depth, 256)

    def forward(k):
        @pl.when(k == 0)
        def _():
            load_gate.wait()
            load_up.wait()

        local_wait(rows.at[k, :, pl.ds(0, half * feat)], sib_recv.at[k])

        def tile(j, carry):
            columns = pl.ds(pl.multiple_of(j * fwd_tile, 128), fwd_tile)
            part[k, :, columns] = jnp.dot(rows[k], w_v[:, columns], preferred_element_type=F32)
            return carry

        lax.fori_loop(0, wide // fwd_tile, tile, 0)
        y_out[k] = part[k, other, :].astype(BF16)
        send(y_out.at[k], y_in.at[k], y1_send, y1_recv.at[k], partner)

    def activate(k):
        local_wait(y_in.at[k], y1_recv.at[k])
        gate = part[k, mine, pl.ds(0, hidden)] + y_in[k, :, pl.ds(0, hidden)].astype(F32)
        up = part[k, mine, pl.ds(hidden, hidden)] + y_in[k, :, pl.ds(hidden, hidden)].astype(F32)
        g = slot_grad[(x + k) % experts].astype(F32)
        sig = jax.nn.sigmoid(gate)
        gs = g * sig
        d_v[k, mine, pl.ds(0, hidden)] = (gs * up * (1.0 + gate * (1.0 - sig))).astype(BF16)
        d_v[k, mine, pl.ds(hidden, hidden)] = (gs * gate).astype(BF16)
        send(d_v.at[k, mine, :], d_v.at[k, mine, :], y2_send, y2_recv.at[k], partner)

    def backward(k):
        local_wait(d_v.at[k, other, :], y2_recv.at[k])

        def tile(j, carry):
            columns = pl.ds(pl.multiple_of(j * dx_tile, 128), dx_tile)
            g_v[k, :, columns] = lax.dot_general(
                d_v[k], w_v[columns, :], (((1,), (1,)), ((), ())), preferred_element_type=F32
            ).astype(BF16)
            return carry

        lax.fori_loop(0, depth // dx_tile, tile, 0)
        for i in range(half):
            column = pl.ds(pl.multiple_of((2 * i + 1 - c) * feat, 128), feat)
            send(
                g_v.at[k, :, column], g_in.at[k, :, pl.ds(i * feat, feat)],
                g_send, g_recv.at[k], sibling,
            )

    dw_tile = tile_of(hidden, 256)

    def weight_piece(p):
        feats = pl.ds(pl.multiple_of(p * feat, 128), feat)
        block = rows[:, :, feats].reshape(experts * 2 * cap, feat)

        def tile(j, carry):
            columns = pl.ds(pl.multiple_of(j * dw_tile, 128), dw_tile)
            dw_v[feats, columns] = lax.dot_general(
                block, d_v[:, :, columns].reshape(experts * 2 * cap, dw_tile),
                (((0,), (0,)), ((), ())), preferred_element_type=F32,
            ).astype(BF16)
            return carry

        lax.fori_loop(0, wide // dw_tile, tile, 0)
        pltpu.make_async_copy(
            dw_v.at[feats, pl.ds(0, hidden)], gate_grad.at[feats, :], dw_sem.at[p, 0]
        ).start()
        pltpu.make_async_copy(
            dw_v.at[feats, pl.ds(hidden, hidden)], up_grad.at[feats, :], dw_sem.at[p, 1]
        ).start()

    at_fwd = chips
    at_y1 = at_fwd + LAG_Y1
    at_y2 = at_y1 + LAG_Y2
    at_rs = at_y2 + LAG_RS
    last = TAU * (experts - 1)
    ticks = last + at_rs + chips
    at_dw = last + at_y2 + 1

    def tick(t, carry):
        def transfers(k, inner):
            u = t - TAU * k
            d = u - at_rs

            @pl.when(d == 0)
            def _():
                local_wait(g_in.at[k], g_recv.at[k])

            @pl.when(jnp.logical_and(d >= 0, d < chips))
            def _():
                reduce_hop(k, d, 0)
                reduce_hop(k, d, 1)

            @pl.when(jnp.logical_and(u >= 0, u < chips))
            def _():
                gather_hop(k, u, 0)
                gather_hop(k, u, 1)

            return inner

        lax.fori_loop(0, experts, transfers, 0)

        def work(k, inner):
            u = t - TAU * k
            pl.when(u == at_y1)(functools.partial(activate, k))
            pl.when(u == at_y2)(functools.partial(backward, k))
            pl.when(u == at_fwd)(functools.partial(forward, k))
            return inner

        lax.fori_loop(0, experts, work, 0)
        p = t - at_dw
        pl.when(jnp.logical_and(p >= 0, p < chips))(functools.partial(weight_piece, p))
        return carry

    lax.fori_loop(0, ticks, tick, 0)

    def late_piece(p, carry):
        weight_piece(p)
        return carry

    lax.fori_loop(max(0, ticks - at_dw), chips, late_piece, 0)

    def returned(k, carry):
        local_wait(ret.at[k], ret_recv.at[k])
        return carry

    lax.fori_loop(0, experts, returned, 0)
    token_grad[...] = jnp.dot(
        token_of[...], ret[...].reshape(experts * cap, feat), preferred_element_type=F32
    ).astype(BF16)

    @pl.when(own)
    def _():
        local_wait(outgoing.at[pl.ds(0, experts - 1)], disp_send)
        local_wait(fin, ret_send)
        local_wait(rs_out.at[:, :, pl.ds(0, half - 1)], rs_send)

    @pl.when(jnp.logical_not(own))
    def _():
        local_wait(outgoing, disp_send)
        local_wait(rs_out, rs_send)

    for sub, after in ((0, (z + 1) % chips), (1, (z + chips - 1) % chips)):
        inside = after // half == r

        @pl.when(inside)
        def _():
            local_wait(rows.at[:, pl.ds(0, cap), pl.ds(0, (half - 1) * feat)], ag_send.at[sub])

        @pl.when(jnp.logical_not(inside))
        def _():
            local_wait(rows.at[:, pl.ds(0, cap), pl.ds(0, half * feat)], ag_send.at[sub])

    local_wait(rows.at[:, :, pl.ds(0, half * feat)], sib_send)
    local_wait(y_out, y1_send)
    local_wait(d_v.at[:, pl.ds(0, cap), :], y2_send)
    local_wait(g_in, g_send)

    def written(p, carry):
        feats = pl.ds(pl.multiple_of(p * feat, 128), feat)
        local_wait(dw_v.at[feats, pl.ds(0, hidden)], dw_sem.at[p, 0])
        local_wait(dw_v.at[feats, pl.ds(hidden, hidden)], dw_sem.at[p, 1])
        return carry

    lax.fori_loop(0, chips, written, 0)


def local(tokens, routes, w_gate, w_up, slot_grad):
    tok_dev, feat = tokens.shape
    experts = lax.axis_size("expert")
    cap = slot_grad.shape[3]
    _, depth, hidden = w_gate.shape
    half = depth // feat // 2
    pairs = routes.reshape(-1)
    onehot = (pairs[:, None] == jnp.arange(experts, dtype=jnp.int32)[None, :]).astype(jnp.int32)
    before = jnp.cumsum(onehot, axis=0) - onehot
    slot = jnp.sum(before * onehot, axis=1)
    target = pairs * cap + slot
    place = (target[:, None] == jnp.arange(experts * cap, dtype=jnp.int32)[None, :]).astype(BF16)
    token_of = place.reshape(tok_dev, routes.shape[1], experts * cap).sum(axis=1)
    outgoing = lax.dot_general(
        token_of, tokens, (((0,), (0,)), ((), ())), preferred_element_type=F32
    )
    outgoing = outgoing.astype(BF16).reshape(experts, cap, feat)
    vmem = pl.BlockSpec(memory_space=pltpu.VMEM)
    hbm = pl.BlockSpec(memory_space=pl.ANY)
    dma = pltpu.SemaphoreType.DMA
    chips = depth // feat
    token_grad, gate_grad, up_grad = pl.pallas_call(
        kernel,
        out_shape=(
            jax.ShapeDtypeStruct((tok_dev, feat), BF16),
            jax.ShapeDtypeStruct((depth, hidden), BF16),
            jax.ShapeDtypeStruct((depth, hidden), BF16),
        ),
        in_specs=[vmem, hbm, hbm, vmem, vmem],
        out_specs=[vmem, hbm, hbm],
        scratch_shapes=[
            pltpu.VMEM((depth, 2 * hidden), BF16),
            pltpu.VMEM((experts, 2 * cap, depth), BF16),
            pltpu.VMEM((experts, 2 * cap, 2 * hidden), F32),
            pltpu.VMEM((experts, cap, 2 * hidden), BF16),
            pltpu.VMEM((experts, cap, 2 * hidden), BF16),
            pltpu.VMEM((experts, 2 * cap, 2 * hidden), BF16),
            pltpu.VMEM((experts, 2 * cap, depth), BF16),
            pltpu.VMEM((experts, 2 * cap, half * feat), BF16),
            pltpu.VMEM((experts, 2, half, cap, feat), BF16),
            pltpu.VMEM((experts, 2, half, cap, feat), BF16),
            pltpu.VMEM((2 * experts - 1, cap, feat), BF16),
            pltpu.VMEM((experts, cap, feat), BF16),
            pltpu.VMEM((depth, 2 * hidden), BF16),
            dma((2,)), dma((chips, 2)),
            dma, dma((experts, 2)),
            dma((2,)), dma((experts, 2, half)),
            dma, dma((experts,)),
            dma, dma((experts,)),
            dma, dma((experts,)),
            dma, dma((experts,)),
            dma, dma((experts, 2, half)),
            dma, dma((experts,)),
        ],
        compiler_params=pltpu.CompilerParams(
            collective_id=0, has_side_effects=True, vmem_limit_bytes=56 * 2**20
        ),
        cost_estimate=pl.CostEstimate(
            flops=3 * 2 * experts * 2 * cap * depth * 2 * hidden,
            bytes_accessed=8 * depth * hidden,
            transcendentals=experts * cap * hidden,
        ),
    )(outgoing, w_gate[0], w_up[0], slot_grad[0, 0], token_of)
    return token_grad, gate_grad[None], up_grad[None]


def solution(mesh):
    in_specs = (
        P(("dp", "expert"), "etp"),
        P(("dp", "expert"), None),
        P("expert", "dp", "etp"),
        P("expert", "dp", "etp"),
        P("dp", "expert", None, None, "etp"),
    )
    out_specs = (P(("dp", "expert"), "etp"), P("expert", "dp", "etp"), P("expert", "dp", "etp"))
    return jax.shard_map(local, mesh=mesh, in_specs=in_specs, out_specs=out_specs, check_vma=False)
```

```python
import functools

import jax
import jax.numpy as jnp
from jax import lax
from jax.experimental import pallas as pl
from jax.experimental.pallas import tpu as pltpu
from jax.sharding import PartitionSpec as P

MESH = pl.DeviceIdType.MESH
F32 = jnp.float32
BF16 = jnp.bfloat16

LAG_ACT = 2
LAG_RS = 1


def tile_of(size, most):
    return most if size % most == 0 else size


def kernel(
    tokens, routes, w_gate, w_up, slot_grad,
    token_grad, gate_grad, up_grad,
    w_v, w_t, token_of, outgoing, rows, part, y_out, y_in, sg_v, d_v, g_v, g_in, rs_out, rs_in, fin, ret, dw_v,
    w_sem, dw_sem, disp_send, disp_recv, ag_send, ag_recv, sib_send, sib_recv,
    sg_send, sg_recv, y_send, y_recv, g_send, g_recv, rs_send, rs_recv, ret_send, ret_recv,
):
    experts, cap, feat = outgoing.shape
    tok_dev = tokens.shape[0]
    depth, hidden = w_gate.shape
    chips = depth // feat
    half = chips // 2
    r = lax.axis_index("dp")
    x = lax.axis_index("expert")
    m = lax.axis_index("etp")
    z = m // 2
    c = m % 2
    i_own = z % half
    across = (z + half) % chips
    h = z // half
    z_from = jnp.where(h == r, z, across)
    alone = jnp.logical_and(r == 0, h == 0)
    up = (r, x, ((z + 1) % chips) * 2 + c)
    down = (r, x, ((z + chips - 1) % chips) * 2 + c)

    def held(k, s):
        return jnp.where(s // half == r, k % 2, 1 - k % 2)

    def target(k):
        return (h, (x + experts - k) % experts, jnp.where(r == k % 2, z, across) * 2 + c)

    def origin(k):
        return (held(k, z), (x + k) % experts, z_from * 2 + c)

    sibling = (r, x, z * 2 + 1 - c)
    partner = (1 - r, x, m)

    def wait(ref, sem):
        pltpu.make_async_copy(ref, ref, sem).wait()

    def send(src, dst, send_sem, recv_sem, device):
        pltpu.make_async_remote_copy(
            src_ref=src, dst_ref=dst, send_sem=send_sem, recv_sem=recv_sem,
            device_id=device, device_id_type=MESH,
        ).start()

    barrier = pltpu.get_barrier_semaphore()

    def greet(k, carry):
        @pl.when(jnp.logical_not(jnp.logical_and(alone, k == 0)))
        def _():
            for device in (target(k), origin(k)):
                pl.semaphore_signal(barrier, inc=1, device_id=device, device_id_type=MESH)

        return carry

    lax.fori_loop(0, experts, greet, 0)
    for device in (up, down, sibling, partner):
        pl.semaphore_signal(barrier, inc=1, device_id=device, device_id_type=MESH)

    load_gate = pltpu.make_async_copy(w_gate, w_v.at[:, pl.ds(0, hidden)], w_sem.at[0])
    load_up = pltpu.make_async_copy(w_up, w_v.at[:, pl.ds(hidden, hidden)], w_sem.at[1])
    load_gate.start()
    load_up.start()
    keep_grad = pltpu.make_async_copy(slot_grad, sg_v.at[r], w_sem.at[2])
    keep_grad.start()

    slots = experts * cap
    place = lax.broadcasted_iota(jnp.int32, (slots, tok_dev), 0)
    expert_of = place // cap
    names = jnp.logical_or(routes[0:1, :] == expert_of, routes[1:2, :] == expert_of)
    earlier = (
        lax.broadcasted_iota(jnp.int32, (tok_dev, tok_dev), 0)
        < lax.broadcasted_iota(jnp.int32, (tok_dev, tok_dev), 1)
    )
    count = jnp.dot(
        names.astype(F32).astype(BF16), earlier.astype(F32).astype(BF16), preferred_element_type=F32
    )
    here = jnp.logical_and(names, count == (place - expert_of * cap).astype(F32))
    token_of[...] = here.astype(F32).astype(BF16)
    outgoing[...] = jnp.dot(
        token_of[...], tokens[...], preferred_element_type=F32
    ).astype(BF16).reshape(experts, cap, feat)

    @pl.when(alone)
    def _():
        pl.semaphore_wait(barrier, 2 * experts + 2)

    @pl.when(jnp.logical_not(alone))
    def _():
        pl.semaphore_wait(barrier, 2 * experts + 4)

    def feats(i, core):
        return pl.ds(pl.multiple_of((2 * i + core) * feat, 128), feat)

    def rows_of(which):
        return pl.ds(pl.multiple_of(which * cap, 16), cap)

    def block_at(k, s):
        return rows.at[k, rows_of(held(k, s)), feats(s % half, c)]

    def dispatch(k, carry):
        there = (x + experts - k) % experts
        dst = rows.at[k, rows_of(r), feats(i_own, c)]
        to_self = jnp.logical_and(alone, k == 0)

        @pl.when(to_self)
        def _():
            pltpu.make_async_copy(outgoing.at[there], dst, disp_recv.at[k]).start()

        @pl.when(jnp.logical_not(to_self))
        def _():
            send(outgoing.at[there], dst, disp_send, disp_recv.at[k], target(k))

        return carry

    lax.fori_loop(0, experts, dispatch, 0)
    send(slot_grad, sg_v.at[r], sg_send, sg_recv, partner)

    def on_ring(k, distance):
        return (z + chips + (1 - 2 * (k % 2)) * distance) % chips

    def beside(k, distance):
        return (r, x, on_ring(k, distance) * 2 + c)

    def gather_step(k, d):
        @pl.when(d == 0)
        def _():
            own = block_at(k, z)
            wait(own, disp_recv.at[k])
            send(own, own, ag_send, ag_recv.at[k, 0, 0], beside(k, 1))
            if half > 1:
                send(own, own, ag_send, ag_recv.at[k, 1, 0], beside(k, -1))
            send(own, own, sib_send, sib_recv.at[k], sibling)

        @pl.when(d > 0)
        def _():
            block = block_at(k, on_ring(k, -d))
            wait(block, ag_recv.at[k, 0, d - 1])

            @pl.when(d < half)
            def _():
                send(block, block, ag_send, ag_recv.at[k, 0, d], beside(k, 1))

            send(block, block, sib_send, sib_recv.at[k], sibling)

        @pl.when(jnp.logical_and(d > 0, d < half))
        def _():
            block = block_at(k, on_ring(k, d))
            wait(block, ag_recv.at[k, 1, d - 1])

            @pl.when(d < half - 1)
            def _():
                send(block, block, ag_send, ag_recv.at[k, 1, d], beside(k, -1))

            send(block, block, sib_send, sib_recv.at[k], sibling)

    def reduce_step(k, d):
        def term(s):
            which = rows_of(held(k, s))
            packed = pl.ds(pl.multiple_of((s % half) * feat, 128), feat)
            return g_v[k, which, feats(s % half, c)].astype(F32) + g_in[k, which, packed].astype(F32)

        @pl.when(d == 0)
        def _():
            wait(g_in.at[k], g_recv.at[k])
            rs_out[k, 0, 0] = term(on_ring(k, half)).astype(BF16)
            send(rs_out.at[k, 0, 0], rs_in.at[k, 0, 0], rs_send, rs_recv.at[k, 0, 0], beside(k, -1))

        @pl.when(jnp.logical_and(d > 0, d < half))
        def _():
            wait(rs_in.at[k, 0, d - 1], rs_recv.at[k, 0, d - 1])
            total = term(on_ring(k, d - half)) + rs_in[k, 0, d - 1].astype(F32)
            rs_out[k, 0, d] = total.astype(BF16)
            send(rs_out.at[k, 0, d], rs_in.at[k, 0, d], rs_send, rs_recv.at[k, 0, d], beside(k, -1))

        @pl.when(jnp.logical_and(d == 1, half > 1))
        def _():
            rs_out[k, 1, 1] = term(on_ring(k, half - 1)).astype(BF16)

        @pl.when(jnp.logical_and(d > 1, d < half))
        def _():
            wait(rs_in.at[k, 1, d - 1], rs_recv.at[k, 1, d - 1])
            total = term(on_ring(k, half - d)) + rs_in[k, 1, d - 1].astype(F32)
            rs_out[k, 1, d] = total.astype(BF16)

        @pl.when(jnp.logical_and(d > 0, d < half))
        def _():
            send(rs_out.at[k, 1, d], rs_in.at[k, 1, d], rs_send, rs_recv.at[k, 1, d], beside(k, 1))

        @pl.when(d == half)
        def _():
            wait(rs_in.at[k, 0, half - 1], rs_recv.at[k, 0, half - 1])
            total = term(z) + rs_in[k, 0, half - 1].astype(F32)
            if half > 1:
                wait(rs_in.at[k, 1, half - 1], rs_recv.at[k, 1, half - 1])
                total = total + rs_in[k, 1, half - 1].astype(F32)
            fin[k] = total.astype(BF16)
            to_self = jnp.logical_and(alone, k == 0)

            @pl.when(to_self)
            def _():
                pltpu.make_async_copy(fin.at[k], ret.at[x], ret_recv.at[x]).start()

            @pl.when(jnp.logical_not(to_self))
            def _():
                send(fin.at[k], ret.at[x], ret_send, ret_recv.at[x], origin(k))

    wide = 2 * hidden
    fwd_tile = tile_of(wide, 512)
    dx_tile = tile_of(depth, 1024)

    load_gate.wait()
    load_up.wait()

    def turn(j, carry):
        columns = pl.ds(pl.multiple_of(j * dx_tile, 128), dx_tile)
        w_t[:, columns] = w_v[columns, :].T
        return carry

    lax.fori_loop(0, depth // dx_tile, turn, 0)

    def forward(k):
        wait(rows.at[k, :, pl.ds(0, half * feat)], sib_recv.at[k])

        def tile(j, carry):
            columns = pl.ds(pl.multiple_of(j * fwd_tile, 128), fwd_tile)
            product = jnp.dot(rows[k], w_v[:, columns], preferred_element_type=F32)
            part[k, :, columns] = product
            y_out[k, :, columns] = product.astype(BF16)
            return carry

        lax.fori_loop(0, wide // fwd_tile, tile, 0)
        send(y_out.at[k], y_in.at[k], y_send, y_recv.at[k], partner)

    def backward(k):
        @pl.when(k == 0)
        def _():
            keep_grad.wait()
            wait(sg_v.at[1 - r], sg_recv)

        wait(y_in.at[k], y_recv.at[k])
        source = (x + k) % experts
        for which in range(2):
            mine = pl.ds(which * cap, cap)
            gate = part[k, mine, pl.ds(0, hidden)] + y_in[k, mine, pl.ds(0, hidden)].astype(F32)
            up_v = part[k, mine, pl.ds(hidden, hidden)] + y_in[k, mine, pl.ds(hidden, hidden)].astype(F32)
            sig = jax.nn.sigmoid(gate)
            gs = sg_v[which, source].astype(F32) * sig
            d_v[k, mine, pl.ds(0, hidden)] = (gs * up_v * (1.0 + gate * (1.0 - sig))).astype(BF16)
            d_v[k, mine, pl.ds(hidden, hidden)] = (gs * gate).astype(BF16)

        def tile(j, carry):
            columns = pl.ds(pl.multiple_of(j * dx_tile, 128), dx_tile)
            g_v[k, :, columns] = jnp.dot(
                d_v[k], w_t[:, columns], preferred_element_type=F32
            ).astype(BF16)
            return carry

        lax.fori_loop(0, depth // dx_tile, tile, 0)
        for i in range(half):
            send(
                g_v.at[k, :, feats(i, 1 - c)], g_in.at[k, :, pl.ds(i * feat, feat)],
                g_send, g_recv.at[k], sibling,
            )

    dw_tile = tile_of(hidden, 256)

    def weight_piece(p):
        here = pl.ds(pl.multiple_of(p * feat, 128), feat)
        block = rows[:, :, here].reshape(experts * 2 * cap, feat)

        def tile(j, carry):
            columns = pl.ds(pl.multiple_of(j * dw_tile, 128), dw_tile)
            dw_v[here, columns] = lax.dot_general(
                block, d_v[:, :, columns].reshape(experts * 2 * cap, dw_tile),
                (((0,), (0,)), ((), ())), preferred_element_type=F32,
            ).astype(BF16)
            return carry

        lax.fori_loop(0, wide // dw_tile, tile, 0)
        pltpu.make_async_copy(
            dw_v.at[here, pl.ds(0, hidden)], gate_grad.at[here, :], dw_sem.at[p, 0]
        ).start()
        pltpu.make_async_copy(
            dw_v.at[here, pl.ds(hidden, hidden)], up_grad.at[here, :], dw_sem.at[p, 1]
        ).start()

    at_fwd = half + 1
    at_act = at_fwd + LAG_ACT
    at_rs = at_act + LAG_RS
    last = experts - 1
    ticks = last + at_rs + half + 1
    at_dw = last + at_act + 1
    per_tick = -(-chips // half)

    def tick(t, carry):
        def transfers(k, inner):
            u = t - k
            d = u - at_rs

            @pl.when(jnp.logical_and(d >= 0, d <= half))
            def _():
                reduce_step(k, d)

            @pl.when(jnp.logical_and(u >= 0, u <= half))
            def _():
                gather_step(k, u)

            return inner

        lax.fori_loop(0, experts, transfers, 0)

        def work(k, inner):
            u = t - k
            pl.when(u == at_act)(functools.partial(backward, k))
            pl.when(u == at_fwd)(functools.partial(forward, k))
            return inner

        lax.fori_loop(0, experts, work, 0)

        def pieces(q, inner):
            p = (t - at_dw) * per_tick + q
            pl.when(jnp.logical_and(p >= 0, p < chips))(functools.partial(weight_piece, p))
            return inner

        lax.fori_loop(0, per_tick, pieces, 0)
        return carry

    lax.fori_loop(0, ticks, tick, 0)

    def returned(k, carry):
        wait(ret.at[k], ret_recv.at[k])
        return carry

    lax.fori_loop(0, experts, returned, 0)
    token_grad[...] = lax.dot_general(
        token_of[...], ret[...].reshape(slots, feat), (((0,), (0,)), ((), ())), preferred_element_type=F32
    ).astype(BF16)

    @pl.when(alone)
    def _():
        wait(outgoing.at[pl.ds(0, experts - 1)], disp_send)
        wait(fin.at[pl.ds(0, experts - 1)], ret_send)

    @pl.when(jnp.logical_not(alone))
    def _():
        wait(outgoing, disp_send)
        wait(fin, ret_send)

    wait(slot_grad, sg_send)
    wait(rows.at[:, pl.ds(0, cap), pl.ds(0, (chips - 1) * feat)], ag_send)
    wait(rows.at[:, :, pl.ds(0, half * feat)], sib_send)
    wait(y_out, y_send)
    wait(g_in, g_send)
    wait(rows.at[:, pl.ds(0, cap), pl.ds(0, (chips - 1) * feat)], rs_send)

    def written(p, carry):
        here = pl.ds(pl.multiple_of(p * feat, 128), feat)
        wait(dw_v.at[here, pl.ds(0, hidden)], dw_sem.at[p, 0])
        wait(dw_v.at[here, pl.ds(hidden, hidden)], dw_sem.at[p, 1])
        return carry

    lax.fori_loop(0, chips, written, 0)


def local(tokens, routes, w_gate, w_up, slot_grad):
    tok_dev, feat = tokens.shape
    experts = lax.axis_size("expert")
    cap = slot_grad.shape[3]
    _, depth, hidden = w_gate.shape
    chips = depth // feat
    half = chips // 2
    vmem = pl.BlockSpec(memory_space=pltpu.VMEM)
    hbm = pl.BlockSpec(memory_space=pl.ANY)
    dma = pltpu.SemaphoreType.DMA
    token_grad, gate_grad, up_grad = pl.pallas_call(
        kernel,
        out_shape=(
            jax.ShapeDtypeStruct((tok_dev, feat), BF16),
            jax.ShapeDtypeStruct((depth, hidden), BF16),
            jax.ShapeDtypeStruct((depth, hidden), BF16),
        ),
        in_specs=[vmem, vmem, hbm, hbm, vmem],
        out_specs=[vmem, hbm, hbm],
        scratch_shapes=[
            pltpu.VMEM((depth, 2 * hidden), BF16),
            pltpu.VMEM((2 * hidden, depth), BF16),
            pltpu.VMEM((experts * cap, tok_dev), BF16),
            pltpu.VMEM((experts, cap, feat), BF16),
            pltpu.VMEM((experts, 2 * cap, depth), BF16),
            pltpu.VMEM((experts, 2 * cap, 2 * hidden), F32),
            pltpu.VMEM((experts, 2 * cap, 2 * hidden), BF16),
            pltpu.VMEM((experts, 2 * cap, 2 * hidden), BF16),
            pltpu.VMEM((2, experts, cap, hidden), BF16),
            pltpu.VMEM((experts, 2 * cap, 2 * hidden), BF16),
            pltpu.VMEM((experts, 2 * cap, depth), BF16),
            pltpu.VMEM((experts, 2 * cap, half * feat), BF16),
            pltpu.VMEM((experts, 2, half, cap, feat), BF16),
            pltpu.VMEM((experts, 2, half, cap, feat), BF16),
            pltpu.VMEM((experts, cap, feat), BF16),
            pltpu.VMEM((experts, cap, feat), BF16),
            pltpu.VMEM((depth, 2 * hidden), BF16),
            dma((3,)), dma((chips, 2)),
            dma, dma((experts,)),
            dma, dma((experts, 2, half)),
            dma, dma((experts,)),
            dma, dma,
            dma, dma((experts,)),
            dma, dma((experts,)),
            dma, dma((experts, 2, half)),
            dma, dma((experts,)),
        ],
        compiler_params=pltpu.CompilerParams(
            collective_id=0, has_side_effects=True, vmem_limit_bytes=56 * 2**20
        ),
        cost_estimate=pl.CostEstimate(
            flops=3 * 2 * experts * 2 * cap * depth * 2 * hidden,
            bytes_accessed=8 * depth * hidden,
            transcendentals=experts * 2 * cap * hidden,
        ),
    )(tokens, routes.T, w_gate[0], w_up[0], slot_grad[0, 0])
    return token_grad, gate_grad[None], up_grad[None]


def solution(mesh):
    in_specs = (
        P(("dp", "expert"), "etp"),
        P(("dp", "expert"), None),
        P("expert", "dp", "etp"),
        P("expert", "dp", "etp"),
        P("dp", "expert", None, None, "etp"),
    )
    out_specs = (P(("dp", "expert"), "etp"), P("expert", "dp", "etp"), P("expert", "dp", "etp"))
    return jax.shard_map(local, mesh=mesh, in_specs=in_specs, out_specs=out_specs, check_vma=False)
```

```python
import functools

import jax
import jax.numpy as jnp
from jax import lax
from jax.experimental import pallas as pl
from jax.experimental.pallas import tpu as pltpu
from jax.sharding import PartitionSpec as P

MESH = pl.DeviceIdType.MESH
F32 = jnp.float32
BF16 = jnp.bfloat16

LAG_ACT = 2
LAG_RS = 1


def tile_of(size, most):
    return most if size % most == 0 else size


def kernel(
    tokens, routes, w_gate, w_up, slot_grad,
    token_grad, weight_grads,
    w_v, w_t, token_of, outgoing, rows, part, y_out, y_in, sg_v, d_v, g_v, g_in, rs_out, rs_in, fin, ret, dw_v,
    w_sem, dw_sem, disp_send, disp_recv, ag_send, ag_recv, sib_send, sib_recv,
    sg_send, sg_recv, y_send, y_recv, g_send, g_recv, rs_send, rs_recv, ret_send, ret_recv,
):
    experts, cap, feat = outgoing.shape
    tok_dev = tokens.shape[0]
    depth, hidden = w_gate.shape
    chips = depth // feat
    half = chips // 2
    r = lax.axis_index("dp")
    x = lax.axis_index("expert")
    m = lax.axis_index("etp")
    z = m // 2
    c = m % 2
    i_own = z % half
    across = chips - 1 - z
    h = z // half
    z_from = jnp.where(h == r, z, across)
    alone = jnp.logical_and(r == 0, h == 0)
    up = (r, x, ((z + 1) % chips) * 2 + c)
    down = (r, x, ((z + chips - 1) % chips) * 2 + c)

    def feature(s):
        return jnp.where(s // half == r, s % half, half - 1 - s % half)

    def held(k, s):
        return jnp.where(s // half == r, k % 2, 1 - k % 2)

    def target(k):
        return (h, (x + experts - k) % experts, jnp.where(r == k % 2, z, across) * 2 + c)

    def origin(k):
        return (held(k, z), (x + k) % experts, z_from * 2 + c)

    sibling = (r, x, z * 2 + 1 - c)
    partner = (1 - r, x, m)

    def wait(ref, sem):
        pltpu.make_async_copy(ref, ref, sem).wait()

    def send(src, dst, send_sem, recv_sem, device):
        pltpu.make_async_remote_copy(
            src_ref=src, dst_ref=dst, send_sem=send_sem, recv_sem=recv_sem,
            device_id=device, device_id_type=MESH,
        ).start()

    barrier = pltpu.get_barrier_semaphore()

    def greet(k, carry):
        @pl.when(jnp.logical_not(jnp.logical_and(alone, k == 0)))
        def _():
            for device in (target(k), origin(k)):
                pl.semaphore_signal(barrier, inc=1, device_id=device, device_id_type=MESH)

        return carry

    lax.fori_loop(0, experts, greet, 0)
    for device in (up, down, sibling, partner):
        pl.semaphore_signal(barrier, inc=1, device_id=device, device_id_type=MESH)

    load_gate = pltpu.make_async_copy(w_gate, w_v.at[:, pl.ds(0, hidden)], w_sem.at[0])
    load_up = pltpu.make_async_copy(w_up, w_v.at[:, pl.ds(hidden, hidden)], w_sem.at[1])
    load_gate.start()
    load_up.start()
    keep_grad = pltpu.make_async_copy(slot_grad, sg_v.at[r], w_sem.at[2])
    keep_grad.start()

    slots = experts * cap
    place = lax.broadcasted_iota(jnp.int32, (slots, tok_dev), 0)
    expert_of = place // cap
    names = jnp.logical_or(routes[0:1, :] == expert_of, routes[1:2, :] == expert_of)
    earlier = (
        lax.broadcasted_iota(jnp.int32, (tok_dev, tok_dev), 0)
        < lax.broadcasted_iota(jnp.int32, (tok_dev, tok_dev), 1)
    )
    count = jnp.dot(
        names.astype(F32).astype(BF16), earlier.astype(F32).astype(BF16), preferred_element_type=F32
    )
    here = jnp.logical_and(names, count == (place - expert_of * cap).astype(F32))
    token_of[...] = here.astype(F32).astype(BF16)
    outgoing[...] = jnp.dot(
        token_of[...], tokens[...], preferred_element_type=F32
    ).astype(BF16).reshape(experts, cap, feat)

    @pl.when(alone)
    def _():
        pl.semaphore_wait(barrier, 2 * experts + 2)

    @pl.when(jnp.logical_not(alone))
    def _():
        pl.semaphore_wait(barrier, 2 * experts + 4)

    def feats(i, core):
        return pl.ds(pl.multiple_of((2 * i + core) * feat, 128), feat)

    def rows_of(which):
        return pl.ds(pl.multiple_of(which * cap, 16), cap)

    def block_at(k, s):
        return rows.at[k, rows_of(held(k, s)), feats(feature(s), c)]

    def dispatch(k, carry):
        there = (x + experts - k) % experts
        dst = rows.at[k, rows_of(r), feats(i_own, c)]
        to_self = jnp.logical_and(alone, k == 0)

        @pl.when(to_self)
        def _():
            pltpu.make_async_copy(outgoing.at[there], dst, disp_recv.at[k]).start()

        @pl.when(jnp.logical_not(to_self))
        def _():
            send(outgoing.at[there], dst, disp_send, disp_recv.at[k], target(k))

        return carry

    lax.fori_loop(0, experts, dispatch, 0)
    send(slot_grad, sg_v.at[r], sg_send, sg_recv, partner)

    def on_ring(k, distance):
        return (z + chips + (1 - 2 * (k % 2)) * distance) % chips

    def beside(k, distance):
        return (r, x, on_ring(k, distance) * 2 + c)

    def gather_step(k, d):
        @pl.when(d == 0)
        def _():
            own = block_at(k, z)
            wait(own, disp_recv.at[k])
            send(own, own, ag_send, ag_recv.at[k, 0, 0], beside(k, 1))
            if half > 1:
                send(own, own, ag_send, ag_recv.at[k, 1, 0], beside(k, -1))
            send(own, own, sib_send, sib_recv.at[k], sibling)

        @pl.when(d > 0)
        def _():
            block = block_at(k, on_ring(k, -d))
            wait(block, ag_recv.at[k, 0, d - 1])

            @pl.when(d < half)
            def _():
                send(block, block, ag_send, ag_recv.at[k, 0, d], beside(k, 1))

            send(block, block, sib_send, sib_recv.at[k], sibling)

        @pl.when(jnp.logical_and(d > 0, d < half))
        def _():
            block = block_at(k, on_ring(k, d))
            wait(block, ag_recv.at[k, 1, d - 1])

            @pl.when(d < half - 1)
            def _():
                send(block, block, ag_send, ag_recv.at[k, 1, d], beside(k, -1))

            send(block, block, sib_send, sib_recv.at[k], sibling)

    def reduce_step(k, d):
        def term(s):
            which = rows_of(held(k, s))
            packed = pl.ds(pl.multiple_of(feature(s) * feat, 128), feat)
            return g_v[k, which, feats(feature(s), c)].astype(F32) + g_in[k, which, packed].astype(F32)

        @pl.when(d == 0)
        def _():
            wait(g_in.at[k], g_recv.at[k])
            rs_out[k, 0, 0] = term(on_ring(k, half)).astype(BF16)
            send(rs_out.at[k, 0, 0], rs_in.at[k, 0, 0], rs_send, rs_recv.at[k, 0, 0], beside(k, -1))

        @pl.when(jnp.logical_and(d > 0, d < half))
        def _():
            wait(rs_in.at[k, 0, d - 1], rs_recv.at[k, 0, d - 1])
            total = term(on_ring(k, d - half)) + rs_in[k, 0, d - 1].astype(F32)
            rs_out[k, 0, d] = total.astype(BF16)
            send(rs_out.at[k, 0, d], rs_in.at[k, 0, d], rs_send, rs_recv.at[k, 0, d], beside(k, -1))

        @pl.when(jnp.logical_and(d == 1, half > 1))
        def _():
            rs_out[k, 1, 1] = term(on_ring(k, half - 1)).astype(BF16)

        @pl.when(jnp.logical_and(d > 1, d < half))
        def _():
            wait(rs_in.at[k, 1, d - 1], rs_recv.at[k, 1, d - 1])
            total = term(on_ring(k, half - d)) + rs_in[k, 1, d - 1].astype(F32)
            rs_out[k, 1, d] = total.astype(BF16)

        @pl.when(jnp.logical_and(d > 0, d < half))
        def _():
            send(rs_out.at[k, 1, d], rs_in.at[k, 1, d], rs_send, rs_recv.at[k, 1, d], beside(k, 1))

        @pl.when(d == half)
        def _():
            wait(rs_in.at[k, 0, half - 1], rs_recv.at[k, 0, half - 1])
            total = term(z) + rs_in[k, 0, half - 1].astype(F32)
            if half > 1:
                wait(rs_in.at[k, 1, half - 1], rs_recv.at[k, 1, half - 1])
                total = total + rs_in[k, 1, half - 1].astype(F32)
            fin[k] = total.astype(BF16)
            to_self = jnp.logical_and(alone, k == 0)

            @pl.when(to_self)
            def _():
                pltpu.make_async_copy(fin.at[k], ret.at[x], ret_recv.at[x]).start()

            @pl.when(jnp.logical_not(to_self))
            def _():
                send(fin.at[k], ret.at[x], ret_send, ret_recv.at[x], origin(k))

    wide = 2 * hidden
    fwd_tile = tile_of(wide, 512)
    dx_tile = tile_of(depth, 1024)

    load_gate.wait()
    load_up.wait()

    def turn(j, carry):
        columns = pl.ds(pl.multiple_of(j * dx_tile, 128), dx_tile)
        w_t[:, columns] = w_v[columns, :].T
        return carry

    lax.fori_loop(0, depth // dx_tile, turn, 0)

    def forward(k):
        wait(rows.at[k, :, pl.ds(0, half * feat)], sib_recv.at[k])

        def tile(j, carry):
            columns = pl.ds(pl.multiple_of(j * fwd_tile, 128), fwd_tile)
            product = jnp.dot(rows[k], w_v[:, columns], preferred_element_type=F32)
            part[k, :, columns] = product
            y_out[k, :, columns] = product.astype(BF16)
            return carry

        lax.fori_loop(0, wide // fwd_tile, tile, 0)
        send(y_out.at[k], y_in.at[k], y_send, y_recv.at[k], partner)

    def backward(k):
        @pl.when(k == 0)
        def _():
            keep_grad.wait()
            wait(sg_v.at[1 - r], sg_recv)

        wait(y_in.at[k], y_recv.at[k])
        source = (x + k) % experts
        for which in range(2):
            mine = pl.ds(which * cap, cap)
            gate = part[k, mine, pl.ds(0, hidden)] + y_in[k, mine, pl.ds(0, hidden)].astype(F32)
            up_v = part[k, mine, pl.ds(hidden, hidden)] + y_in[k, mine, pl.ds(hidden, hidden)].astype(F32)
            sig = jax.nn.sigmoid(gate)
            gs = sg_v[which, source].astype(F32) * sig
            d_v[k, mine, pl.ds(0, hidden)] = (gs * up_v * (1.0 + gate * (1.0 - sig))).astype(BF16)
            d_v[k, mine, pl.ds(hidden, hidden)] = (gs * gate).astype(BF16)

        def tile(j, carry):
            columns = pl.ds(pl.multiple_of(j * dx_tile, 128), dx_tile)
            g_v[k, :, columns] = jnp.dot(
                d_v[k], w_t[:, columns], preferred_element_type=F32
            ).astype(BF16)
            return carry

        lax.fori_loop(0, depth // dx_tile, tile, 0)
        for i in range(half):
            send(
                g_v.at[k, :, feats(i, 1 - c)], g_in.at[k, :, pl.ds(i * feat, feat)],
                g_send, g_recv.at[k], sibling,
            )

    dw_tile = tile_of(hidden, 256)

    def weight_piece(p):
        here = pl.ds(pl.multiple_of(p * feat, 128), feat)
        block = rows[:, :, here].reshape(experts * 2 * cap, feat)

        def tile(j, carry):
            columns = pl.ds(pl.multiple_of(j * dw_tile, 128), dw_tile)
            dw_v[here, columns] = lax.dot_general(
                block, d_v[:, :, columns].reshape(experts * 2 * cap, dw_tile),
                (((0,), (0,)), ((), ())), preferred_element_type=F32,
            ).astype(BF16)
            return carry

        lax.fori_loop(0, wide // dw_tile, tile, 0)
        pltpu.make_async_copy(
            dw_v.at[here, pl.ds(0, hidden)], weight_grads.at[0, here, :], dw_sem.at[p, 0]
        ).start()
        pltpu.make_async_copy(
            dw_v.at[here, pl.ds(hidden, hidden)], weight_grads.at[1, here, :], dw_sem.at[p, 1]
        ).start()

    at_fwd = half + 1
    at_act = at_fwd + LAG_ACT
    at_rs = at_act + LAG_RS
    last = experts - 1
    ticks = last + at_rs + half + 1
    at_dw = last + at_act + 1
    per_tick = -(-chips // half)

    def tick(t, carry):
        def transfers(k, inner):
            u = t - k
            d = u - at_rs

            @pl.when(jnp.logical_and(d >= 0, d <= half))
            def _():
                reduce_step(k, d)

            @pl.when(jnp.logical_and(u >= 0, u <= half))
            def _():
                gather_step(k, u)

            return inner

        lax.fori_loop(0, experts, transfers, 0)

        def work(k, inner):
            u = t - k
            pl.when(u == at_act)(functools.partial(backward, k))
            pl.when(u == at_fwd)(functools.partial(forward, k))
            return inner

        lax.fori_loop(0, experts, work, 0)

        def pieces(q, inner):
            p = (t - at_dw) * per_tick + q
            pl.when(jnp.logical_and(p >= 0, p < chips))(functools.partial(weight_piece, p))
            return inner

        lax.fori_loop(0, per_tick, pieces, 0)
        return carry

    lax.fori_loop(0, ticks, tick, 0)

    def returned(k, carry):
        wait(ret.at[k], ret_recv.at[k])
        return carry

    lax.fori_loop(0, experts, returned, 0)
    token_grad[...] = lax.dot_general(
        token_of[...], ret[...].reshape(slots, feat), (((0,), (0,)), ((), ())), preferred_element_type=F32
    ).astype(BF16)

    @pl.when(alone)
    def _():
        wait(outgoing.at[pl.ds(0, experts - 1)], disp_send)
        wait(fin.at[pl.ds(0, experts - 1)], ret_send)

    @pl.when(jnp.logical_not(alone))
    def _():
        wait(outgoing, disp_send)
        wait(fin, ret_send)

    wait(slot_grad, sg_send)
    wait(rows.at[:, pl.ds(0, cap), pl.ds(0, (chips - 1) * feat)], ag_send)
    wait(rows.at[:, :, pl.ds(0, half * feat)], sib_send)
    wait(y_out, y_send)
    wait(g_in, g_send)
    wait(rows.at[:, pl.ds(0, cap), pl.ds(0, (chips - 1) * feat)], rs_send)

    def written(p, carry):
        here = pl.ds(pl.multiple_of(p * feat, 128), feat)
        wait(dw_v.at[here, pl.ds(0, hidden)], dw_sem.at[p, 0])
        wait(dw_v.at[here, pl.ds(hidden, hidden)], dw_sem.at[p, 1])
        return carry

    lax.fori_loop(0, chips, written, 0)


def local(tokens, routes, w_gate, w_up, slot_grad):
    tok_dev, feat = tokens.shape
    experts = lax.axis_size("expert")
    cap = slot_grad.shape[3]
    _, depth, hidden = w_gate.shape
    chips = depth // feat
    half = chips // 2
    vmem = pl.BlockSpec(memory_space=pltpu.VMEM)
    hbm = pl.BlockSpec(memory_space=pl.ANY)
    dma = pltpu.SemaphoreType.DMA
    token_grad, weight_grads = pl.pallas_call(
        kernel,
        out_shape=(
            jax.ShapeDtypeStruct((tok_dev, feat), BF16),
            jax.ShapeDtypeStruct((2, depth, hidden), BF16),
        ),
        in_specs=[vmem, vmem, hbm, hbm, vmem],
        out_specs=[vmem, hbm],
        scratch_shapes=[
            pltpu.VMEM((depth, 2 * hidden), BF16),
            pltpu.VMEM((2 * hidden, depth), BF16),
            pltpu.VMEM((experts * cap, tok_dev), BF16),
            pltpu.VMEM((experts, cap, feat), BF16),
            pltpu.VMEM((experts, 2 * cap, depth), BF16),
            pltpu.VMEM((experts, 2 * cap, 2 * hidden), F32),
            pltpu.VMEM((experts, 2 * cap, 2 * hidden), BF16),
            pltpu.VMEM((experts, 2 * cap, 2 * hidden), BF16),
            pltpu.VMEM((2, experts, cap, hidden), BF16),
            pltpu.VMEM((experts, 2 * cap, 2 * hidden), BF16),
            pltpu.VMEM((experts, 2 * cap, depth), BF16),
            pltpu.VMEM((experts, 2 * cap, half * feat), BF16),
            pltpu.VMEM((experts, 2, half, cap, feat), BF16),
            pltpu.VMEM((experts, 2, half, cap, feat), BF16),
            pltpu.VMEM((experts, cap, feat), BF16),
            pltpu.VMEM((experts, cap, feat), BF16),
            pltpu.VMEM((depth, 2 * hidden), BF16),
            dma((3,)), dma((chips, 2)),
            dma, dma((experts,)),
            dma, dma((experts, 2, half)),
            dma, dma((experts,)),
            dma, dma,
            dma, dma((experts,)),
            dma, dma((experts,)),
            dma, dma((experts, 2, half)),
            dma, dma((experts,)),
        ],
        compiler_params=pltpu.CompilerParams(
            collective_id=0, has_side_effects=True, vmem_limit_bytes=56 * 2**20
        ),
        cost_estimate=pl.CostEstimate(
            flops=3 * 2 * experts * 2 * cap * depth * 2 * hidden,
            bytes_accessed=8 * depth * hidden,
            transcendentals=experts * 2 * cap * hidden,
        ),
    )(tokens, routes.T, w_gate[0], w_up[0], slot_grad[0, 0])
    return token_grad, weight_grads[0:1], weight_grads[1:2]


def solution(mesh):
    in_specs = (
        P(("dp", "expert"), "etp"),
        P(("dp", "expert"), None),
        P("expert", "dp", "etp"),
        P("expert", "dp", "etp"),
        P("dp", "expert", None, None, "etp"),
    )
    out_specs = (P(("dp", "expert"), "etp"), P("expert", "dp", "etp"), P("expert", "dp", "etp"))
    return jax.shard_map(local, mesh=mesh, in_specs=in_specs, out_specs=out_specs, check_vma=False)
```

```python
import functools

import jax
import jax.numpy as jnp
from jax import lax
from jax.experimental import pallas as pl
from jax.experimental.pallas import tpu as pltpu
from jax.sharding import PartitionSpec as P

MESH = pl.DeviceIdType.MESH
F32 = jnp.float32
BF16 = jnp.bfloat16

LAG_ACT = 2
LAG_RS = 1
GRAD_TICK = 1


def tile_of(size, most):
    return most if size % most == 0 else size


def kernel(
    tokens, routes, w_gate, w_up, slot_grad,
    token_grad, weight_grads,
    w_v, w_t, token_of, outgoing, rows, part, y_out, y_in, sg_v, d_v, g_v, g_in, rs_out, rs_in, fin, ret, dw_v,
    w_sem, dw_sem, disp_send, disp_recv, ag_send, ag_recv, sib_send, sib_recv,
    sg_send, sg_recv, y_send, y_recv, g_send, g_recv, rs_send, rs_recv, ret_send, ret_recv,
):
    experts, cap, feat = outgoing.shape
    tok_dev = tokens.shape[0]
    depth, hidden = w_gate.shape
    chips = depth // feat
    half = chips // 2
    r = lax.axis_index("dp")
    x = lax.axis_index("expert")
    m = lax.axis_index("etp")
    z = m // 2
    c = m % 2
    i_own = z % half
    across = chips - 1 - z
    h = z // half
    z_from = jnp.where(h == r, z, across)
    alone = jnp.logical_and(r == 0, h == 0)
    up = (r, x, ((z + 1) % chips) * 2 + c)
    down = (r, x, ((z + chips - 1) % chips) * 2 + c)

    def feature(s):
        return jnp.where(s // half == r, s % half, half - 1 - s % half)

    def held(k, s):
        return jnp.where(s // half == r, k % 2, 1 - k % 2)

    def target(k):
        return (h, (x + experts - k) % experts, jnp.where(r == k % 2, z, across) * 2 + c)

    def origin(k):
        return (held(k, z), (x + k) % experts, z_from * 2 + c)

    sibling = (r, x, z * 2 + 1 - c)
    partner = (1 - r, x, m)

    def wait(ref, sem):
        pltpu.make_async_copy(ref, ref, sem).wait()

    def send(src, dst, send_sem, recv_sem, device):
        pltpu.make_async_remote_copy(
            src_ref=src, dst_ref=dst, send_sem=send_sem, recv_sem=recv_sem,
            device_id=device, device_id_type=MESH,
        ).start()

    barrier = pltpu.get_barrier_semaphore()

    def greet(k, carry):
        @pl.when(jnp.logical_not(jnp.logical_and(alone, k == 0)))
        def _():
            for device in (target(k), origin(k)):
                pl.semaphore_signal(barrier, inc=1, device_id=device, device_id_type=MESH)

        return carry

    lax.fori_loop(0, experts, greet, 0)
    for device in (up, down, sibling, partner):
        pl.semaphore_signal(barrier, inc=1, device_id=device, device_id_type=MESH)

    load_gate = pltpu.make_async_copy(w_gate, w_v.at[:, pl.ds(0, hidden)], w_sem.at[0])
    load_up = pltpu.make_async_copy(w_up, w_v.at[:, pl.ds(hidden, hidden)], w_sem.at[1])
    load_gate.start()
    load_up.start()
    keep_grad = pltpu.make_async_copy(slot_grad, sg_v.at[r], w_sem.at[2])
    keep_grad.start()

    slots = experts * cap
    place = lax.broadcasted_iota(jnp.int32, (slots, tok_dev), 0)
    expert_of = place // cap
    names = jnp.logical_or(routes[0:1, :] == expert_of, routes[1:2, :] == expert_of)
    earlier = (
        lax.broadcasted_iota(jnp.int32, (tok_dev, tok_dev), 0)
        < lax.broadcasted_iota(jnp.int32, (tok_dev, tok_dev), 1)
    )
    count = jnp.dot(
        names.astype(F32).astype(BF16), earlier.astype(F32).astype(BF16), preferred_element_type=F32
    )
    here = jnp.logical_and(names, count == (place - expert_of * cap).astype(F32))
    token_of[...] = here.astype(F32).astype(BF16)
    outgoing[...] = jnp.dot(
        token_of[...], tokens[...], preferred_element_type=F32
    ).astype(BF16).reshape(experts, cap, feat)

    @pl.when(alone)
    def _():
        pl.semaphore_wait(barrier, 2 * experts + 2)

    @pl.when(jnp.logical_not(alone))
    def _():
        pl.semaphore_wait(barrier, 2 * experts + 4)

    def feats(i, core):
        return pl.ds(pl.multiple_of((2 * i + core) * feat, 128), feat)

    def rows_of(which):
        return pl.ds(pl.multiple_of(which * cap, 16), cap)

    def block_at(k, s):
        return rows.at[k, rows_of(held(k, s)), feats(feature(s), c)]

    def dispatch(k, carry):
        there = (x + experts - k) % experts
        dst = rows.at[k, rows_of(r), feats(i_own, c)]
        to_self = jnp.logical_and(alone, k == 0)

        @pl.when(to_self)
        def _():
            pltpu.make_async_copy(outgoing.at[there], dst, disp_recv.at[k]).start()

        @pl.when(jnp.logical_not(to_self))
        def _():
            send(outgoing.at[there], dst, disp_send, disp_recv.at[k], target(k))

        return carry

    lax.fori_loop(0, experts, dispatch, 0)

    def on_ring(k, distance):
        return (z + chips + (1 - 2 * (k % 2)) * distance) % chips

    def beside(k, distance):
        return (r, x, on_ring(k, distance) * 2 + c)

    def gather_step(k, d):
        @pl.when(d == 0)
        def _():
            own = block_at(k, z)
            wait(own, disp_recv.at[k])
            send(own, own, ag_send, ag_recv.at[k, 0, 0], beside(k, 1))
            if half > 1:
                send(own, own, ag_send, ag_recv.at[k, 1, 0], beside(k, -1))
            send(own, own, sib_send, sib_recv.at[k], sibling)

        @pl.when(d > 0)
        def _():
            block = block_at(k, on_ring(k, -d))
            wait(block, ag_recv.at[k, 0, d - 1])

            @pl.when(d < half)
            def _():
                send(block, block, ag_send, ag_recv.at[k, 0, d], beside(k, 1))

            send(block, block, sib_send, sib_recv.at[k], sibling)

        @pl.when(jnp.logical_and(d > 0, d < half))
        def _():
            block = block_at(k, on_ring(k, d))
            wait(block, ag_recv.at[k, 1, d - 1])

            @pl.when(d < half - 1)
            def _():
                send(block, block, ag_send, ag_recv.at[k, 1, d], beside(k, -1))

            send(block, block, sib_send, sib_recv.at[k], sibling)

    def reduce_step(k, d):
        def term(s):
            which = rows_of(held(k, s))
            packed = pl.ds(pl.multiple_of(feature(s) * feat, 128), feat)
            return g_v[k, which, feats(feature(s), c)].astype(F32) + g_in[k, which, packed].astype(F32)

        @pl.when(d == 0)
        def _():
            wait(g_in.at[k], g_recv.at[k])
            rs_out[k, 0, 0] = term(on_ring(k, half)).astype(BF16)
            send(rs_out.at[k, 0, 0], rs_in.at[k, 0, 0], rs_send, rs_recv.at[k, 0, 0], beside(k, -1))

        @pl.when(jnp.logical_and(d > 0, d < half))
        def _():
            wait(rs_in.at[k, 0, d - 1], rs_recv.at[k, 0, d - 1])
            total = term(on_ring(k, d - half)) + rs_in[k, 0, d - 1].astype(F32)
            rs_out[k, 0, d] = total.astype(BF16)
            send(rs_out.at[k, 0, d], rs_in.at[k, 0, d], rs_send, rs_recv.at[k, 0, d], beside(k, -1))

        @pl.when(jnp.logical_and(d == 1, half > 1))
        def _():
            rs_out[k, 1, 1] = term(on_ring(k, half - 1)).astype(BF16)

        @pl.when(jnp.logical_and(d > 1, d < half))
        def _():
            wait(rs_in.at[k, 1, d - 1], rs_recv.at[k, 1, d - 1])
            total = term(on_ring(k, half - d)) + rs_in[k, 1, d - 1].astype(F32)
            rs_out[k, 1, d] = total.astype(BF16)

        @pl.when(jnp.logical_and(d > 0, d < half))
        def _():
            send(rs_out.at[k, 1, d], rs_in.at[k, 1, d], rs_send, rs_recv.at[k, 1, d], beside(k, 1))

        @pl.when(d == half)
        def _():
            wait(rs_in.at[k, 0, half - 1], rs_recv.at[k, 0, half - 1])
            total = term(z) + rs_in[k, 0, half - 1].astype(F32)
            if half > 1:
                wait(rs_in.at[k, 1, half - 1], rs_recv.at[k, 1, half - 1])
                total = total + rs_in[k, 1, half - 1].astype(F32)
            fin[k] = total.astype(BF16)
            to_self = jnp.logical_and(alone, k == 0)

            @pl.when(to_self)
            def _():
                pltpu.make_async_copy(fin.at[k], ret.at[x], ret_recv.at[x]).start()

            @pl.when(jnp.logical_not(to_self))
            def _():
                send(fin.at[k], ret.at[x], ret_send, ret_recv.at[x], origin(k))

    wide = 2 * hidden
    fwd_tile = tile_of(wide, 512)
    dx_tile = tile_of(depth, 1024)

    load_gate.wait()
    load_up.wait()

    def turn(j, carry):
        columns = pl.ds(pl.multiple_of(j * dx_tile, 128), dx_tile)
        w_t[:, columns] = w_v[columns, :].T
        return carry

    lax.fori_loop(0, depth // dx_tile, turn, 0)

    def forward(k):
        wait(rows.at[k, :, pl.ds(0, half * feat)], sib_recv.at[k])

        def tile(j, carry):
            columns = pl.ds(pl.multiple_of(j * fwd_tile, 128), fwd_tile)
            product = jnp.dot(rows[k], w_v[:, columns], preferred_element_type=F32)
            part[k, :, columns] = product
            y_out[k, :, columns] = product.astype(BF16)
            send(y_out.at[k, :, columns], y_in.at[k, :, columns], y_send, y_recv.at[k], partner)
            return carry

        lax.fori_loop(0, wide // fwd_tile, tile, 0)

    def backward(k):
        @pl.when(k == 0)
        def _():
            keep_grad.wait()
            wait(sg_v.at[1 - r], sg_recv)

        wait(y_in.at[k], y_recv.at[k])
        source = (x + k) % experts
        for which in range(2):
            mine = pl.ds(which * cap, cap)
            gate = part[k, mine, pl.ds(0, hidden)] + y_in[k, mine, pl.ds(0, hidden)].astype(F32)
            up_v = part[k, mine, pl.ds(hidden, hidden)] + y_in[k, mine, pl.ds(hidden, hidden)].astype(F32)
            sig = jax.nn.sigmoid(gate)
            gs = sg_v[which, source].astype(F32) * sig
            d_v[k, mine, pl.ds(0, hidden)] = (gs * up_v * (1.0 + gate * (1.0 - sig))).astype(BF16)
            d_v[k, mine, pl.ds(hidden, hidden)] = (gs * gate).astype(BF16)

        def tile(j, carry):
            columns = pl.ds(pl.multiple_of(j * dx_tile, 128), dx_tile)
            g_v[k, :, columns] = jnp.dot(
                d_v[k], w_t[:, columns], preferred_element_type=F32
            ).astype(BF16)
            return carry

        lax.fori_loop(0, depth // dx_tile, tile, 0)
        for i in range(half):
            send(
                g_v.at[k, :, feats(i, 1 - c)], g_in.at[k, :, pl.ds(i * feat, feat)],
                g_send, g_recv.at[k], sibling,
            )

    dw_tile = tile_of(hidden, 256)

    def weight_piece(p):
        here = pl.ds(pl.multiple_of(p * feat, 128), feat)
        block = rows[:, :, here].reshape(experts * 2 * cap, feat)

        def tile(j, carry):
            columns = pl.ds(pl.multiple_of(j * dw_tile, 128), dw_tile)
            dw_v[here, columns] = lax.dot_general(
                block, d_v[:, :, columns].reshape(experts * 2 * cap, dw_tile),
                (((0,), (0,)), ((), ())), preferred_element_type=F32,
            ).astype(BF16)
            return carry

        lax.fori_loop(0, wide // dw_tile, tile, 0)
        pltpu.make_async_copy(
            dw_v.at[here, pl.ds(0, hidden)], weight_grads.at[0, here, :], dw_sem.at[p, 0]
        ).start()
        pltpu.make_async_copy(
            dw_v.at[here, pl.ds(hidden, hidden)], weight_grads.at[1, here, :], dw_sem.at[p, 1]
        ).start()

    at_fwd = half + 1
    at_act = at_fwd + LAG_ACT
    at_rs = at_act + LAG_RS
    last = experts - 1
    ticks = last + at_rs + half + 1
    at_dw = last + at_act + 1
    per_tick = -(-chips // half)

    def tick(t, carry):
        @pl.when(t == GRAD_TICK)
        def _():
            send(slot_grad, sg_v.at[r], sg_send, sg_recv, partner)

        def transfers(k, inner):
            u = t - k
            d = u - at_rs

            @pl.when(jnp.logical_and(d >= 0, d <= half))
            def _():
                reduce_step(k, d)

            @pl.when(jnp.logical_and(u >= 0, u <= half))
            def _():
                gather_step(k, u)

            return inner

        lax.fori_loop(0, experts, transfers, 0)

        def work(k, inner):
            u = t - k
            pl.when(u == at_act)(functools.partial(backward, k))
            pl.when(u == at_fwd)(functools.partial(forward, k))
            return inner

        lax.fori_loop(0, experts, work, 0)

        def pieces(q, inner):
            p = (t - at_dw) * per_tick + q
            pl.when(jnp.logical_and(p >= 0, p < chips))(functools.partial(weight_piece, p))
            return inner

        lax.fori_loop(0, per_tick, pieces, 0)
        return carry

    lax.fori_loop(0, ticks, tick, 0)

    def returned(k, carry):
        wait(ret.at[k], ret_recv.at[k])
        return carry

    lax.fori_loop(0, experts, returned, 0)
    token_grad[...] = lax.dot_general(
        token_of[...], ret[...].reshape(slots, feat), (((0,), (0,)), ((), ())), preferred_element_type=F32
    ).astype(BF16)

    @pl.when(alone)
    def _():
        wait(outgoing.at[pl.ds(0, experts - 1)], disp_send)
        wait(fin.at[pl.ds(0, experts - 1)], ret_send)

    @pl.when(jnp.logical_not(alone))
    def _():
        wait(outgoing, disp_send)
        wait(fin, ret_send)

    wait(slot_grad, sg_send)
    wait(rows.at[:, pl.ds(0, cap), pl.ds(0, (chips - 1) * feat)], ag_send)
    wait(rows.at[:, :, pl.ds(0, half * feat)], sib_send)
    wait(y_out, y_send)
    wait(g_in, g_send)
    wait(rows.at[:, pl.ds(0, cap), pl.ds(0, (chips - 1) * feat)], rs_send)

    def written(p, carry):
        here = pl.ds(pl.multiple_of(p * feat, 128), feat)
        wait(dw_v.at[here, pl.ds(0, hidden)], dw_sem.at[p, 0])
        wait(dw_v.at[here, pl.ds(hidden, hidden)], dw_sem.at[p, 1])
        return carry

    lax.fori_loop(0, chips, written, 0)


def local(tokens, routes, w_gate, w_up, slot_grad):
    tok_dev, feat = tokens.shape
    experts = lax.axis_size("expert")
    cap = slot_grad.shape[3]
    _, depth, hidden = w_gate.shape
    chips = depth // feat
    half = chips // 2
    vmem = pl.BlockSpec(memory_space=pltpu.VMEM)
    hbm = pl.BlockSpec(memory_space=pl.ANY)
    dma = pltpu.SemaphoreType.DMA
    token_grad, weight_grads = pl.pallas_call(
        kernel,
        out_shape=(
            jax.ShapeDtypeStruct((tok_dev, feat), BF16),
            jax.ShapeDtypeStruct((2, depth, hidden), BF16),
        ),
        in_specs=[vmem, vmem, hbm, hbm, vmem],
        out_specs=[vmem, hbm],
        scratch_shapes=[
            pltpu.VMEM((depth, 2 * hidden), BF16),
            pltpu.VMEM((2 * hidden, depth), BF16),
            pltpu.VMEM((experts * cap, tok_dev), BF16),
            pltpu.VMEM((experts, cap, feat), BF16),
            pltpu.VMEM((experts, 2 * cap, depth), BF16),
            pltpu.VMEM((experts, 2 * cap, 2 * hidden), F32),
            pltpu.VMEM((experts, 2 * cap, 2 * hidden), BF16),
            pltpu.VMEM((experts, 2 * cap, 2 * hidden), BF16),
            pltpu.VMEM((2, experts, cap, hidden), BF16),
            pltpu.VMEM((experts, 2 * cap, 2 * hidden), BF16),
            pltpu.VMEM((experts, 2 * cap, depth), BF16),
            pltpu.VMEM((experts, 2 * cap, half * feat), BF16),
            pltpu.VMEM((experts, 2, half, cap, feat), BF16),
            pltpu.VMEM((experts, 2, half, cap, feat), BF16),
            pltpu.VMEM((experts, cap, feat), BF16),
            pltpu.VMEM((experts, cap, feat), BF16),
            pltpu.VMEM((depth, 2 * hidden), BF16),
            dma((3,)), dma((chips, 2)),
            dma, dma((experts,)),
            dma, dma((experts, 2, half)),
            dma, dma((experts,)),
            dma, dma,
            dma, dma((experts,)),
            dma, dma((experts,)),
            dma, dma((experts, 2, half)),
            dma, dma((experts,)),
        ],
        compiler_params=pltpu.CompilerParams(
            collective_id=0, has_side_effects=True, vmem_limit_bytes=56 * 2**20
        ),
        cost_estimate=pl.CostEstimate(
            flops=3 * 2 * experts * 2 * cap * depth * 2 * hidden,
            bytes_accessed=8 * depth * hidden,
            transcendentals=experts * 2 * cap * hidden,
        ),
    )(tokens, routes.T, w_gate[0], w_up[0], slot_grad[0, 0])
    return token_grad, weight_grads[0:1], weight_grads[1:2]


def solution(mesh):
    in_specs = (
        P(("dp", "expert"), "etp"),
        P(("dp", "expert"), None),
        P("expert", "dp", "etp"),
        P("expert", "dp", "etp"),
        P("dp", "expert", None, None, "etp"),
    )
    out_specs = (P(("dp", "expert"), "etp"), P("expert", "dp", "etp"), P("expert", "dp", "etp"))
    return jax.shard_map(local, mesh=mesh, in_specs=in_specs, out_specs=out_specs, check_vma=False)
```
